32 devices in a mesh: dp: 8 (over z, y), tensor: 4 (over x, core).
Axes of the slice: x: 2, y: 2, z: 4, core: 2. Of those that a mesh axis runs over, the one named last changes fastest.
Arguments:
- hidden: bfloat16 [1536, 14336], P('dp', 'tensor'), may hold values from -0.15625 to 0.15625
- out_grad: bfloat16 [1536, 8192], P(('dp', 'tensor')), may hold values from -6 to 6
- weights: bfloat16 [4, 32, 128, 128], P('tensor'), may hold values from -0.125 to 0.125
- block_rows: int32 [4, 32], P('tensor'), may hold values from 0 to 27, as said below
- block_cols: int32 [4, 32], P('tensor'), may hold values from 0 to 63, as said below
- counts: int32 [4], P('tensor'), may hold values from 16 to 32, as said below
Outputs:
- weight_grad: float32 [4, 32, 128, 128], P('tensor', 'dp')
- input_grad: bfloat16 [1536, 14336], P('dp', 'tensor')
The draws below stay inside these ranges and needn't reach their ends.
Inputs may be any that keep to these rules, and one draw needn't show every extreme that they name: `block_rows`: within one member, no two slots name the same pair of block row and block column. `block_cols`: pairs with block_rows as stated there. `counts`: some member has all 32 slots live.
All inputs are finite; a program needn't handle non-finite values.
Results may differ from the reference program's by a relative error of at most 0.001.
Values may be sent and summed in bfloat16 or wider, within the bound.
A program may use at most 128 MiB of HBM per device.

```python
import jax
import jax.numpy as jnp
from jax import lax

D = 8192
FF = 14336
BLK = 128
SLOTS = 32
TOKENS = 1536
PANEL = 28
NBC = 64
N_TENSOR = 4


def block_cells(key):
    member_keys = jax.random.split(jax.random.fold_in(key, 11), N_TENSOR)
    orders = jax.vmap(lambda single: jax.random.permutation(single, PANEL * NBC))(member_keys)
    return orders[:, :SLOTS].astype(jnp.int32)


def draw_block_rows(key, part):
    return block_cells(key) // NBC


def draw_block_cols(key, part):
    return block_cells(key) % NBC


def draw_counts(key, part):
    values = jax.random.randint(jax.random.fold_in(key, 5), (N_TENSOR,), SLOTS // 2, SLOTS + 1)
    fullest = jax.random.randint(jax.random.fold_in(key, 6), (), 0, N_TENSOR)
    return values.at[fullest].set(SLOTS).astype(jnp.int32)


def block_scale(stream_key, extent, pieces, smallest, top_value):
    level = 1.0
    for dim, parts in pieces:
        heights = jax.random.uniform(jax.random.fold_in(jax.random.fold_in(stream_key, 6), dim), (parts,), jnp.float32, smallest / len(pieces), top_value / len(pieces))
        level = level * jnp.repeat(jnp.exp(heights), extent[dim] // parts).reshape((-1,) + (1,) * (len(extent) - 1 - dim))
    return level


def gaussian(key, shape, spread, bound, shards=(), held_as=jnp.bfloat16):
    gain = block_scale(key, shape, shards, -0.22, 0.18) if shards else 1.0
    result = jax.random.normal(key, shape, jnp.float32) * spread * gain
    return jnp.minimum(jnp.maximum(result, -bound), bound).astype(held_as)


def setup_inputs(seed: int = 0) -> dict:
    key_list = jax.random.split(jax.random.key(seed), 7)
    return {
        "hidden": gaussian(key_list[0], (TOKENS, FF), (TOKENS ** -0.5), 0.15625, ((0, 8), (1, 4))),
        "out_grad": gaussian(key_list[1], (TOKENS, D), 1.0, 6.0, ((0, 32),)),
        "weights": gaussian(key_list[2], (N_TENSOR, SLOTS, BLK, BLK), (D // 4) ** -0.5, 0.125, ((0, 4),)),
        "block_rows": draw_block_rows(jax.random.fold_in(key_list[6], 71), 0),
        "block_cols": draw_block_cols(jax.random.fold_in(key_list[6], 71), 0),
        "counts": draw_counts(jax.random.fold_in(key_list[6], 71), 0),
    }


def member_terms(member, hidden, out_grad, weights, block_rows, block_cols, counts):
    width = hidden.shape[1] // N_TENSOR
    act_panel = lax.dynamic_slice_in_dim(hidden, member * width, width, 1)
    own_weights = weights[member]
    own_rows = block_rows[member]
    own_cols = block_cols[member]
    active_count = counts[member]

    def slot_step(running_totals, position_slot):
        starting_row = (own_rows[position_slot] * BLK).astype(jnp.int32)
        col_start = (own_cols[position_slot] * BLK).astype(jnp.int32)
        active_flags = (position_slot < active_count).astype(jnp.float32)
        activation_block = lax.dynamic_slice_in_dim(act_panel, starting_row, BLK, 1)
        gradient_block = lax.dynamic_slice_in_dim(out_grad, col_start, BLK, 1)
        block_gradient = jnp.dot(activation_block.T, gradient_block, preferred_element_type=jnp.float32) * active_flags
        contribution = jnp.dot(gradient_block, own_weights[position_slot].T, preferred_element_type=jnp.float32)
        preceding_count = lax.dynamic_slice_in_dim(running_totals, starting_row, BLK, 1)
        running_totals = lax.dynamic_update_slice_in_dim(running_totals, preceding_count + active_flags * contribution, starting_row, 1)
        return running_totals, block_gradient

    initial = jnp.zeros((hidden.shape[0], width), jnp.float32)
    running_totals, grads = lax.scan(slot_step, initial, jnp.arange(SLOTS, dtype=jnp.int32))
    return running_totals.astype(jnp.bfloat16), grads


def reference(hidden, out_grad, weights, block_rows, block_cols, counts):
    def one_member(member):
        return member_terms(member, hidden, out_grad, weights, block_rows, block_cols, counts)

    panels, weight_grad = lax.map(one_member, jnp.arange(N_TENSOR, dtype=jnp.int32))
    input_grad = jnp.transpose(panels, (1, 0, 2)).reshape(hidden.shape[0], hidden.shape[1])
    return weight_grad, input_grad
```

```python
import functools

import jax
import jax.numpy as jnp
from jax import lax
from jax.experimental import pallas as pl
from jax.experimental.pallas import tpu as pltpu
from jax.sharding import PartitionSpec as P

MESH = pl.DeviceIdType.MESH


def kernel(
    n_t,
    n_dp,
    per,
    panel,
    meta,
    cols_ref,
    hid_hbm,
    og_hbm,
    w_hbm,
    wg_out,
    ig_out,
    hid,
    og,
    w,
    allcols,
    cols_sm,
    sbuf,
    gbuf,
    part,
    recv,
    runs,
    ig,
    in_sem,
    sm_sem,
    c_send,
    c_recv,
    g_send,
    g_recv,
    r_send,
    r_recv,
    out_sem,
):
    slots = per * n_dp
    rows = og.shape[1]
    blk = w.shape[1]
    stages = n_dp.bit_length() - 1
    me_t = lax.axis_index("tensor")
    me_d = lax.axis_index("dp")

    w_in = pltpu.make_async_copy(w_hbm, w, in_sem.at[2])

    def load(src, dst, sem):
        def one(c, carry):
            columns = pl.ds(pl.multiple_of(c * blk, blk), blk)
            pltpu.make_async_copy(src.at[:, columns], dst.at[c], sem).start()
            return carry

        lax.fori_loop(0, dst.shape[0], one, 0)

    load(og_hbm, og, in_sem.at[0])

    def peer(r):
        return lax.rem(me_t + r, n_t)

    def source(r):
        return lax.rem(me_t + n_t - r, n_t)

    def bit(b):
        return lax.rem(me_d // (1 << b), 2)

    def partner(b):
        return me_d + (1 << b) * (1 - 2 * bit(b))

    barrier = pltpu.get_barrier_semaphore()
    for r in range(1, n_t):
        pl.semaphore_signal(barrier, inc=1, device_id={"tensor": peer(r)}, device_id_type=MESH)
    for b in range(stages):
        pl.semaphore_signal(barrier, inc=1, device_id={"dp": partner(b)}, device_id_type=MESH)
    pl.semaphore_wait(barrier, n_t - 1 + stages)

    col_copies = []
    for r in range(1, n_t):
        copy = pltpu.make_async_remote_copy(
            src_ref=cols_ref,
            dst_ref=allcols.at[r],
            send_sem=c_send.at[r],
            recv_sem=c_recv.at[r],
            device_id={"tensor": peer(r)},
            device_id_type=MESH,
        )
        copy.start()
        col_copies.append(copy)
    own_cols = pltpu.make_async_copy(cols_ref, cols_sm.at[0], sm_sem.at[0])
    own_cols.start()
    load(hid_hbm, hid, in_sem.at[1])
    w_in.start()
    runs[slots] = jnp.zeros(runs.shape[1:], jnp.float32)
    for r in range(1, n_t):
        col_copies[r - 1].wait_recv()
        pltpu.make_async_copy(allcols.at[r], cols_sm.at[r], sm_sem.at[r]).start()
    for r in range(1, n_t):
        pltpu.make_async_copy(allcols.at[r], cols_sm.at[r], sm_sem.at[r]).wait()
    own_cols.wait()
    pltpu.make_async_copy(og, og, in_sem.at[0]).wait()

    def gather_copy(r, j):
        return pltpu.make_async_remote_copy(
            src_ref=sbuf.at[r, pl.ds(j * n_dp, n_dp)],
            dst_ref=gbuf.at[pl.ds(j * n_dp, n_dp), pl.ds(pl.multiple_of(me_t * rows, 16), rows)],
            send_sem=g_send.at[r, j],
            recv_sem=g_recv.at[r, j],
            device_id={"tensor": peer(r)},
            device_id_type=MESH,
        )

    def block_of(r, k):
        return og[cols_sm[r, 0, k]]

    order = sorted(range(1, n_t), key=lambda r: -min(r, n_t - r))
    for j in range(per):
        for r in order:

            def pick(q, carry, r=r, j=j):
                sbuf[r, j * n_dp + q] = block_of(n_t - r, j * n_dp + q)
                return carry

            lax.fori_loop(0, n_dp, pick, 0)
            gather_copy(r, j).start()

    def own(k, carry):
        gbuf[k, pl.ds(pl.multiple_of(me_t * rows, 16), rows)] = block_of(0, k)
        return carry

    lax.fori_loop(0, slots, own, 0)
    pltpu.make_async_copy(hid, hid, in_sem.at[1]).wait()
    w_in.wait()

    def base(level):
        first = 0
        for b in range(level):
            first = first + bit(b) * (n_dp >> (b + 1))
        return first

    def offset(b):
        return sum(n_dp >> (i + 1) for i in range(b))

    def reduce_copy(j, b):
        half = n_dp >> (b + 1)
        return pltpu.make_async_remote_copy(
            src_ref=part.at[j, pl.ds(base(b) + (1 - bit(b)) * half, half)],
            dst_ref=recv.at[j, pl.ds(offset(b), half)],
            send_sem=r_send.at[j, b],
            recv_sem=r_recv.at[j, b],
            device_id={"dp": partner(b)},
            device_id_type=MESH,
        )

    def slot_of(j, q):
        d = 0
        for b in range(stages):
            d = d + lax.rem(q // (1 << b), 2) * (n_dp >> (b + 1))
        return d * per + j

    def products(j, first, count):
        def one(i, carry):
            q = first + i
            k = j * n_dp + q
            h = hid[meta[k]]
            part[j, q] = lax.dot_general(
                h, gbuf[k], (((0,), (0,)), ((), ())), preferred_element_type=jnp.float32
            )
            return carry

        lax.fori_loop(0, count, one, 0)

    def contributions(j):
        def one(q, carry):
            k = j * n_dp + q
            c = lax.dot_general(
                gbuf[k], w[slot_of(j, q)], (((1,), (1,)), ((), ())), preferred_element_type=jnp.float32
            )
            runs[k] = c + runs[meta[slots + k]]
            return carry

        lax.fori_loop(0, n_dp, one, 0)

    def first_half(j):
        for r in range(1, n_t):
            gather_copy(r, j).wait_recv()
        half = n_dp // 2
        products(j, (1 - bit(0)) * half, half)
        reduce_copy(j, 0).start()
        products(j, bit(0) * half, half)
        contributions(j)

    def advance(j, b):
        half = n_dp >> (b + 1)
        reduce_copy(j, b).wait_recv()
        mine = base(b + 1)

        def add(i, carry):
            part[j, mine + i] = part[j, mine + i] + recv[j, offset(b) + i]
            return carry

        lax.fori_loop(0, half, add, 0)
        if b + 1 < stages:
            reduce_copy(j, b + 1).start()

    def write_out():
        for p in range(panel):
            ig[:, p * blk : (p + 1) * blk] = runs[meta[2 * slots + p]].astype(ig.dtype)

    ig_copy = pltpu.make_async_copy(ig, ig_out, out_sem.at[0])
    for step in range(per + stages):
        if step < per:
            first_half(step)
        if step == per - 1:
            write_out()
            ig_copy.start()
        for b in reversed(range(stages)):
            j = step - 1 - b
            if 0 <= j < per:
                advance(j, b)
    wg_copies = []
    for j in range(per):
        copy = pltpu.make_async_copy(part.at[j, base(stages)], wg_out.at[j], out_sem.at[1 + j])
        copy.start()
        wg_copies.append(copy)
    for r in range(1, n_t):
        col_copies[r - 1].wait_send()
        for j in range(per):
            gather_copy(r, j).wait_send()
    for j in range(per):
        for b in range(stages):
            reduce_copy(j, b).wait_send()
        wg_copies[j].wait()
    ig_copy.wait()


def shards(n_t, n_dp, hidden, out_grad, weights, block_rows, block_cols, counts):
    w = weights[0]
    slots, blk, _ = w.shape
    tokens, width = hidden.shape
    rows = out_grad.shape[0]
    panel = width // blk
    per = slots // n_dp
    stages = n_dp.bit_length() - 1

    def arranged(a):
        return a.reshape((2,) * stages + (per,)).transpose(*reversed(range(stages + 1))).reshape(slots)

    rows_k = arranged(block_rows[0])
    cols_k = arranged(block_cols[0])
    live_k = arranged(jnp.arange(slots, dtype=jnp.int32)) < counts[0]
    index = jnp.arange(slots, dtype=jnp.int32)
    wanted = jnp.concatenate([rows_k, jnp.arange(panel, dtype=jnp.int32)])
    limit = jnp.concatenate([index, jnp.full((panel,), slots, jnp.int32)])
    match = (wanted[:, None] == rows_k[None, :]) & live_k[None, :] & (index[None, :] < limit[:, None])
    found = jnp.max(jnp.where(match, index[None, :], -1), axis=1)
    meta = jnp.concatenate([rows_k, jnp.where(found < 0, slots, found)])
    cols = jnp.pad(cols_k[None, :], ((0, 0), (0, 128 - slots)))

    anyspace = pl.BlockSpec(memory_space=pl.ANY)
    flops = 4 * slots * tokens * blk * blk
    wg, ig = pl.pallas_call(
        functools.partial(kernel, n_t, n_dp, per, panel),
        out_shape=(
            jax.ShapeDtypeStruct((per, blk, blk), jnp.float32),
            jax.ShapeDtypeStruct((tokens, width), jnp.bfloat16),
        ),
        in_specs=[
            pl.BlockSpec(memory_space=pltpu.SMEM),
            pl.BlockSpec(memory_space=pltpu.VMEM),
            anyspace,
            anyspace,
            anyspace,
        ],
        out_specs=(anyspace, anyspace),
        scratch_shapes=[
            pltpu.VMEM((panel, tokens, blk), jnp.bfloat16),
            pltpu.VMEM((out_grad.shape[1] // blk, rows, blk), jnp.bfloat16),
            pltpu.VMEM(w.shape, jnp.bfloat16),
            pltpu.VMEM((n_t, 1, 128), jnp.int32),
            pltpu.SMEM((n_t, 1, 128), jnp.int32),
            pltpu.VMEM((n_t, slots, rows, blk), jnp.bfloat16),
            pltpu.VMEM((slots, tokens, blk), jnp.bfloat16),
            pltpu.VMEM((per, n_dp, blk, blk), jnp.float32),
            pltpu.VMEM((per, n_dp, blk, blk), jnp.float32),
            pltpu.VMEM((slots + 1, tokens, blk), jnp.float32),
            pltpu.VMEM((tokens, width), jnp.bfloat16),
            pltpu.SemaphoreType.DMA((3,)),
            pltpu.SemaphoreType.DMA((n_t,)),
            pltpu.SemaphoreType.DMA((n_t,)),
            pltpu.SemaphoreType.DMA((n_t,)),
            pltpu.SemaphoreType.DMA((n_t, per)),
            pltpu.SemaphoreType.DMA((n_t, per)),
            pltpu.SemaphoreType.DMA((per, stages)),
            pltpu.SemaphoreType.DMA((per, stages)),
            pltpu.SemaphoreType.DMA((1 + per,)),
        ],
        compiler_params=pltpu.CompilerParams(
            collective_id=0, has_side_effects=True, vmem_limit_bytes=52 * 2**20
        ),
        cost_estimate=pl.CostEstimate(flops=flops, bytes_accessed=6 * 2**20, transcendentals=0),
    )(meta, cols, hidden, out_grad, w)
    live = lax.axis_index("dp") * per + jnp.arange(per, dtype=jnp.int32) < counts[0]
    return jnp.where(live[:, None, None], wg, 0.0)[None], ig


def solution(mesh):
    in_specs = (
        P("dp", "tensor"),
        P(("dp", "tensor"), None),
        P("tensor", None, None, None),
        P("tensor", None),
        P("tensor", None),
        P("tensor"),
    )
    out_specs = (P("tensor", "dp", None, None), P("dp", "tensor"))
    body = functools.partial(shards, mesh.shape["tensor"], mesh.shape["dp"])
    return jax.shard_map(body, mesh=mesh, in_specs=in_specs, out_specs=out_specs, check_vma=False)
```

```python
import functools

import jax
import jax.numpy as jnp
from jax import lax
from jax.experimental import pallas as pl
from jax.experimental.pallas import tpu as pltpu
from jax.sharding import PartitionSpec as P

MESH = pl.DeviceIdType.MESH


def kernel(
    n_t,
    n_dp,
    per,
    panel,
    counts,
    rows_ref,
    cols_ref,
    hid_hbm,
    og_hbm,
    w_hbm,
    wg_out,
    ig_out,
    hid,
    og,
    w,
    allcols,
    cols_sm,
    key,
    before,
    last,
    sbuf,
    gbuf,
    part,
    recv,
    runs,
    ig,
    in_sem,
    sm_sem,
    c_send,
    c_recv,
    g_send,
    g_recv,
    r_send,
    r_recv,
    out_sem,
):
    slots = per * n_dp
    rows = og.shape[1]
    blk = w.shape[1]
    stages = n_dp.bit_length() - 1
    me_t = lax.axis_index("tensor")
    me_d = lax.axis_index("dp")

    w_in = pltpu.make_async_copy(w_hbm, w, in_sem.at[2])

    def load(src, dst, sem):
        def one(c, carry):
            columns = pl.ds(pl.multiple_of(c * blk, blk), blk)
            pltpu.make_async_copy(src.at[:, columns], dst.at[c], sem).start()
            return carry

        lax.fori_loop(0, dst.shape[0], one, 0)

    load(og_hbm, og, in_sem.at[0])

    def peer(r):
        return lax.rem(me_t + r, n_t)

    def source(r):
        return lax.rem(me_t + n_t - r, n_t)

    def bit(b):
        return lax.rem(me_d // (1 << b), 2)

    def bits(j):
        listed = list(range(stages))
        if j % 4 == 1 and stages > 1:
            listed[:2] = [1, 0]
        return listed

    def slot_of(j, q):
        d = 0
        for level, b in enumerate(bits(j)):
            d = d + lax.rem(q // (n_dp >> (level + 1)), 2) * (1 << b)
        return d * per + j

    def partner(b):
        return me_d + (1 << b) * (1 - 2 * bit(b))

    barrier = pltpu.get_barrier_semaphore()
    for r in range(1, n_t):
        pl.semaphore_signal(barrier, inc=1, device_id={"tensor": peer(r)}, device_id_type=MESH)
    for b in range(stages):
        pl.semaphore_signal(barrier, inc=1, device_id={"dp": partner(b)}, device_id_type=MESH)
    pl.semaphore_wait(barrier, n_t - 1 + stages)

    col_copies = []
    for r in range(1, n_t):
        copy = pltpu.make_async_remote_copy(
            src_ref=cols_ref,
            dst_ref=allcols.at[r],
            send_sem=c_send.at[r],
            recv_sem=c_recv.at[r],
            device_id={"tensor": peer(r)},
            device_id_type=MESH,
        )
        copy.start()
        col_copies.append(copy)
    own_cols = pltpu.make_async_copy(cols_ref, cols_sm.at[0], sm_sem.at[0])
    own_cols.start()
    load(hid_hbm, hid, in_sem.at[1])
    w_in.start()
    runs[slots] = jnp.zeros(runs.shape[1:], jnp.float32)
    for r in range(1, n_t):
        col_copies[r - 1].wait_recv()
        pltpu.make_async_copy(allcols.at[r], cols_sm.at[r], sm_sem.at[r]).start()
    for r in range(1, n_t):
        pltpu.make_async_copy(allcols.at[r], cols_sm.at[r], sm_sem.at[r]).wait()
    own_cols.wait()
    pltpu.make_async_copy(og, og, in_sem.at[0]).wait()

    def gather_copy(r, j):
        return pltpu.make_async_remote_copy(
            src_ref=sbuf.at[r, pl.ds(j * n_dp, n_dp)],
            dst_ref=gbuf.at[pl.ds(j * n_dp, n_dp), pl.ds(pl.multiple_of(me_t * rows, 16), rows)],
            send_sem=g_send.at[r, j],
            recv_sem=g_recv.at[r, j],
            device_id={"tensor": peer(r)},
            device_id_type=MESH,
        )

    def block_of(r, j, q):
        return og[cols_sm[r, 0, slot_of(j, q)]]

    order = sorted(range(1, n_t), key=lambda r: -min(r, n_t - r))
    for j in range(per):
        for r in order:

            def pick(q, carry, r=r, j=j):
                sbuf[r, j * n_dp + q] = block_of(n_t - r, j, q)
                return carry

            lax.fori_loop(0, n_dp, pick, 0, unroll=min(n_dp, 8))
            gather_copy(r, j).start()

    for j in range(per):

        def own(q, carry, j=j):
            gbuf[j * n_dp + q, pl.ds(pl.multiple_of(me_t * rows, 16), rows)] = block_of(0, j, q)
            return carry

        lax.fori_loop(0, n_dp, own, 0, unroll=min(n_dp, 8))

    for j in range(per):

        def mark(q, carry, j=j):
            slot = slot_of(j, q)
            key[j * n_dp + q] = jnp.where(slot < counts[0], rows_ref[0, slot], -1)
            return carry

        lax.fori_loop(0, n_dp, mark, 0, unroll=min(n_dp, 8))

    def find_before(k, carry):
        found = slots
        for k2 in range(slots):
            found = jnp.where((key[k2] == key[k]) & (k2 < k), k2, found)
        before[k] = found
        return carry

    lax.fori_loop(0, slots, find_before, 0)

    def find_last(p, carry):
        found = slots
        for k2 in range(slots):
            found = jnp.where(key[k2] == p, k2, found)
        last[p] = found
        return carry

    lax.fori_loop(0, panel, find_last, 0)
    pltpu.make_async_copy(hid, hid, in_sem.at[1]).wait()
    w_in.wait()

    def base(j, level):
        first = 0
        for i, b in enumerate(bits(j)[:level]):
            first = first + bit(b) * (n_dp >> (i + 1))
        return first

    def offset(b):
        return sum(n_dp >> (i + 1) for i in range(b))

    def reduce_copy(j, level):
        half = n_dp >> (level + 1)
        b = bits(j)[level]
        return pltpu.make_async_remote_copy(
            src_ref=part.at[j, pl.ds(base(j, level) + (1 - bit(b)) * half, half)],
            dst_ref=recv.at[j, pl.ds(offset(level), half)],
            send_sem=r_send.at[j, level],
            recv_sem=r_recv.at[j, level],
            device_id={"dp": partner(b)},
            device_id_type=MESH,
        )

    def products(j, first, count):
        def one(i, carry):
            q = first + i
            h = hid[rows_ref[0, slot_of(j, q)]]
            part[j, q] = lax.dot_general(
                h, gbuf[j * n_dp + q], (((0,), (0,)), ((), ())), preferred_element_type=jnp.float32
            )
            return carry

        lax.fori_loop(0, count, one, 0, unroll=min(count, 4))

    def contributions(j):
        def one(q, carry):
            k = j * n_dp + q
            c = lax.dot_general(
                gbuf[k], w[slot_of(j, q)], (((1,), (1,)), ((), ())), preferred_element_type=jnp.float32
            )
            runs[k] = c + runs[before[k]]
            return carry

        lax.fori_loop(0, n_dp, one, 0, unroll=min(n_dp, 4))

    def first_half(j):
        for r in range(1, n_t):
            gather_copy(r, j).wait_recv()
        half = n_dp // 2
        mine = bit(bits(j)[0]) * half
        products(j, half - mine, half)
        reduce_copy(j, 0).start()
        products(j, mine, half)

    def advance(j, level):
        half = n_dp >> (level + 1)
        reduce_copy(j, level).wait_recv()
        mine = base(j, level + 1)

        def add(i, carry):
            part[j, mine + i] = part[j, mine + i] + recv[j, offset(level) + i]
            return carry

        lax.fori_loop(0, half, add, 0)
        if level + 1 < stages:
            reduce_copy(j, level + 1).start()

    def write_out():
        for p in range(panel):
            ig[:, p * blk : (p + 1) * blk] = runs[last[p]].astype(ig.dtype)

    ig_copy = pltpu.make_async_copy(ig, ig_out, out_sem.at[0])
    for step in range(per + stages):
        if step < per:
            first_half(step)
        if step == per - 1:
            for j in range(per // 2):
                contributions(j)
        for level in reversed(range(stages)):
            j = step - 1 - level
            if 0 <= j < per:
                advance(j, level)
        if step == per - 1:
            for j in range(per // 2, per):
                contributions(j)
            write_out()
            ig_copy.start()
    wg_copies = []
    for j in range(per):
        copy = pltpu.make_async_copy(part.at[j, base(j, stages)], wg_out.at[j], out_sem.at[1 + j])
        copy.start()
        wg_copies.append(copy)
    for r in range(1, n_t):
        col_copies[r - 1].wait_send()
        for j in range(per):
            gather_copy(r, j).wait_send()
    for j in range(per):
        for b in range(stages):
            reduce_copy(j, b).wait_send()
        wg_copies[j].wait()
    ig_copy.wait()


def shards(n_t, n_dp, hidden, out_grad, weights, block_rows, block_cols, counts):
    w = weights[0]
    slots, blk, _ = w.shape
    tokens, width = hidden.shape
    rows = out_grad.shape[0]
    panel = width // blk
    per = slots // n_dp
    stages = n_dp.bit_length() - 1
    anyspace = pl.BlockSpec(memory_space=pl.ANY)
    hbm = pl.BlockSpec(memory_space=pltpu.HBM)
    flops = 4 * slots * tokens * blk * blk
    wg, ig = pl.pallas_call(
        functools.partial(kernel, n_t, n_dp, per, panel),
        out_shape=(
            jax.ShapeDtypeStruct((per, blk, blk), jnp.float32),
            jax.ShapeDtypeStruct((tokens, width), jnp.bfloat16),
        ),
        in_specs=[
            pl.BlockSpec(memory_space=pltpu.SMEM),
            pl.BlockSpec(memory_space=pltpu.SMEM),
            pl.BlockSpec(memory_space=pltpu.VMEM),
            hbm,
            hbm,
            hbm,
        ],
        out_specs=(anyspace, anyspace),
        scratch_shapes=[
            pltpu.VMEM((panel, tokens, blk), jnp.bfloat16),
            pltpu.VMEM((out_grad.shape[1] // blk, rows, blk), jnp.bfloat16),
            pltpu.VMEM(w.shape, jnp.bfloat16),
            pltpu.VMEM((n_t, 1, slots), jnp.int32),
            pltpu.SMEM((n_t, 1, slots), jnp.int32),
            pltpu.SMEM((slots,), jnp.int32),
            pltpu.SMEM((slots,), jnp.int32),
            pltpu.SMEM((panel,), jnp.int32),
            pltpu.VMEM((n_t, slots, rows, blk), jnp.bfloat16),
            pltpu.VMEM((slots, tokens, blk), jnp.bfloat16),
            pltpu.VMEM((per, n_dp, blk, blk), jnp.float32),
            pltpu.VMEM((per, n_dp, blk, blk), jnp.float32),
            pltpu.VMEM((slots + 1, tokens, blk), jnp.float32),
            pltpu.VMEM((tokens, width), jnp.bfloat16),
            pltpu.SemaphoreType.DMA((3,)),
            pltpu.SemaphoreType.DMA((n_t,)),
            pltpu.SemaphoreType.DMA((n_t,)),
            pltpu.SemaphoreType.DMA((n_t,)),
            pltpu.SemaphoreType.DMA((n_t, per)),
            pltpu.SemaphoreType.DMA((n_t, per)),
            pltpu.SemaphoreType.DMA((per, stages)),
            pltpu.SemaphoreType.DMA((per, stages)),
            pltpu.SemaphoreType.DMA((1 + per,)),
        ],
        compiler_params=pltpu.CompilerParams(
            collective_id=0, has_side_effects=True, vmem_limit_bytes=64 * 2**20 - 720 * 2**10
        ),
        cost_estimate=pl.CostEstimate(flops=flops, bytes_accessed=6 * 2**20, transcendentals=0),
    )(counts, block_rows, block_cols, hidden, out_grad, w)
    live = lax.axis_index("dp") * per + jnp.arange(per, dtype=jnp.int32) < counts[0]
    return jnp.where(live[:, None, None], wg, 0.0)[None], ig


def solution(mesh):
    in_specs = (
        P("dp", "tensor"),
        P(("dp", "tensor"), None),
        P("tensor", None, None, None),
        P("tensor", None),
        P("tensor", None),
        P("tensor"),
    )
    out_specs = (P("tensor", "dp", None, None), P("dp", "tensor"))
    body = functools.partial(shards, mesh.shape["tensor"], mesh.shape["dp"])
    return jax.shard_map(body, mesh=mesh, in_specs=in_specs, out_specs=out_specs, check_vma=False)
```

```python
import functools
import math

import jax
import jax.numpy as jnp
from jax import lax
from jax.experimental import pallas as pl
from jax.experimental.pallas import tpu as pltpu
from jax.sharding import PartitionSpec as P

MESH = pl.DeviceIdType.MESH


def kernel(
    n_t,
    n_dp,
    per,
    panel,
    counts,
    rows_ref,
    cols_ref,
    hid_hbm,
    og_hbm,
    w_hbm,
    wg_out,
    ig_out,
    hid,
    og,
    w,
    allcols,
    cols_sm,
    key,
    before,
    last,
    sbuf,
    gbuf,
    part,
    recv,
    runs,
    ig,
    in_sem,
    sm_sem,
    c_send,
    c_recv,
    g_send,
    g_recv,
    r_send,
    r_recv,
    out_sem,
):
    slots = per * n_dp
    rows = og.shape[1]
    blk = w.shape[1]
    stages = n_dp.bit_length() - 1
    me_t = lax.axis_index("tensor")
    me_d = lax.axis_index("dp")

    w_in = pltpu.make_async_copy(w_hbm, w, in_sem.at[2])

    def load(src, dst, sem):
        def one(c, carry):
            columns = pl.ds(pl.multiple_of(c * blk, blk), blk)
            pltpu.make_async_copy(src.at[:, columns], dst.at[c], sem).start()
            return carry

        lax.fori_loop(0, dst.shape[0], one, 0, unroll=math.gcd(dst.shape[0], 16))

    load(og_hbm, og, in_sem.at[0])

    def peer(r):
        return lax.rem(me_t + r, n_t)

    def source(r):
        return lax.rem(me_t + n_t - r, n_t)

    def bit(b):
        return lax.rem(me_d // (1 << b), 2)

    def bits(j):
        listed = list(range(stages))
        if j % 4 == 1 and stages > 1:
            listed[:2] = [1, 0]
        return listed

    def slot_of(j, q):
        d = 0
        for level, b in enumerate(bits(j)):
            d = d + lax.rem(q // (n_dp >> (level + 1)), 2) * (1 << b)
        return d * per + j

    def partner(b):
        return me_d + (1 << b) * (1 - 2 * bit(b))

    barrier = pltpu.get_barrier_semaphore()
    for r in range(1, n_t):
        pl.semaphore_signal(barrier, inc=1, device_id={"tensor": peer(r)}, device_id_type=MESH)
    for b in range(stages):
        pl.semaphore_signal(barrier, inc=1, device_id={"dp": partner(b)}, device_id_type=MESH)
    pl.semaphore_wait(barrier, n_t - 1 + stages)

    col_copies = []
    for r in range(1, n_t):
        copy = pltpu.make_async_remote_copy(
            src_ref=cols_ref,
            dst_ref=allcols.at[r],
            send_sem=c_send.at[r],
            recv_sem=c_recv.at[r],
            device_id={"tensor": peer(r)},
            device_id_type=MESH,
        )
        copy.start()
        col_copies.append(copy)
    own_cols = pltpu.make_async_copy(cols_ref, cols_sm.at[0], sm_sem.at[0])
    own_cols.start()
    load(hid_hbm, hid, in_sem.at[1])
    w_in.start()
    runs[slots] = jnp.zeros(runs.shape[1:], jnp.float32)
    for r in range(1, n_t):
        col_copies[r - 1].wait_recv()
        pltpu.make_async_copy(allcols.at[r], cols_sm.at[r], sm_sem.at[r]).start()
    for r in range(1, n_t):
        pltpu.make_async_copy(allcols.at[r], cols_sm.at[r], sm_sem.at[r]).wait()
    own_cols.wait()
    pltpu.make_async_copy(og, og, in_sem.at[0]).wait()

    def gather_copy(r, j):
        return pltpu.make_async_remote_copy(
            src_ref=sbuf.at[r, pl.ds(j * n_dp, n_dp)],
            dst_ref=gbuf.at[pl.ds(j * n_dp, n_dp), pl.ds(pl.multiple_of(me_t * rows, 16), rows)],
            send_sem=g_send.at[r, j],
            recv_sem=g_recv.at[r, j],
            device_id={"tensor": peer(r)},
            device_id_type=MESH,
        )

    def block_of(r, j, q):
        return og[cols_sm[r, 0, slot_of(j, q)]]

    order = sorted(range(1, n_t), key=lambda r: -min(r, n_t - r))
    for j in range(per):
        for r in order:

            def pick(q, carry, r=r, j=j):
                sbuf[r, j * n_dp + q] = block_of(n_t - r, j, q)
                return carry

            lax.fori_loop(0, n_dp, pick, 0, unroll=min(n_dp, 8))
            gather_copy(r, j).start()

    for j in range(per):

        def own(q, carry, j=j):
            gbuf[j * n_dp + q, pl.ds(pl.multiple_of(me_t * rows, 16), rows)] = block_of(0, j, q)
            return carry

        lax.fori_loop(0, n_dp, own, 0, unroll=min(n_dp, 8))

    pltpu.make_async_copy(hid, hid, in_sem.at[1]).wait()
    w_in.wait()

    def base(j, level):
        first = 0
        for i, b in enumerate(bits(j)[:level]):
            first = first + bit(b) * (n_dp >> (i + 1))
        return first

    def offset(b):
        return sum(n_dp >> (i + 1) for i in range(b))

    def reduce_copy(j, level):
        half = n_dp >> (level + 1)
        b = bits(j)[level]
        return pltpu.make_async_remote_copy(
            src_ref=part.at[j, pl.ds(base(j, level) + (1 - bit(b)) * half, half)],
            dst_ref=recv.at[j, pl.ds(offset(level), half)],
            send_sem=r_send.at[j, level],
            recv_sem=r_recv.at[j, level],
            device_id={"dp": partner(b)},
            device_id_type=MESH,
        )

    def products(j, first, count):
        def one(i, carry):
            q = first + i
            h = hid[rows_ref[0, slot_of(j, q)]]
            part[j, q] = lax.dot_general(
                h, gbuf[j * n_dp + q], (((0,), (0,)), ((), ())), preferred_element_type=jnp.float32
            )
            return carry

        lax.fori_loop(0, count, one, 0, unroll=min(count, 4))

    def contributions(j):
        def one(q, carry):
            k = j * n_dp + q
            c = lax.dot_general(
                gbuf[k], w[slot_of(j, q)], (((1,), (1,)), ((), ())), preferred_element_type=jnp.float32
            )
            runs[k] = c + runs[before[k]]
            return carry

        lax.fori_loop(0, n_dp, one, 0, unroll=min(n_dp, 4))

    def first_half(j):
        for r in range(1, n_t):
            gather_copy(r, j).wait_recv()
        half = n_dp // 2
        mine = bit(bits(j)[0]) * half
        products(j, half - mine, half)
        reduce_copy(j, 0).start()
        products(j, mine, half)

    def advance(j, level):
        half = n_dp >> (level + 1)
        reduce_copy(j, level).wait_recv()
        mine = base(j, level + 1)

        def add(i, carry):
            part[j, mine + i] = part[j, mine + i] + recv[j, offset(level) + i]
            return carry

        lax.fori_loop(0, half, add, 0, unroll=min(half, 4))
        if level + 1 < stages:
            reduce_copy(j, level + 1).start()

    def search():
        for j in range(per):

            def mark(q, carry, j=j):
                slot = slot_of(j, q)
                key[j * n_dp + q] = jnp.where(slot < counts[0], rows_ref[0, slot], -1)
                return carry

            lax.fori_loop(0, n_dp, mark, 0, unroll=min(n_dp, 8))

        def find_before(k, carry):
            found = slots
            for k2 in range(slots):
                found = jnp.where((key[k2] == key[k]) & (k2 < k), k2, found)
            before[k] = found
            return carry

        lax.fori_loop(0, slots, find_before, 0)

        def find_last(p, carry):
            found = slots
            for k2 in range(slots):
                found = jnp.where(key[k2] == p, k2, found)
            last[p] = found
            return carry

        lax.fori_loop(0, panel, find_last, 0)

    def write_out():
        for p in range(panel):
            ig[:, p * blk : (p + 1) * blk] = runs[last[p]].astype(ig.dtype)

    ig_copy = pltpu.make_async_copy(ig, ig_out, out_sem.at[0])
    for step in range(per + stages):
        if step < per:
            first_half(step)
        if step == 0:
            search()
        if step == per - 1:
            for j in range(per // 2):
                contributions(j)
        for level in reversed(range(stages)):
            j = step - 1 - level
            if 0 <= j < per:
                advance(j, level)
        if step == per - 1:
            for j in range(per // 2, per):
                contributions(j)
            write_out()
            ig_copy.start()
    wg_copies = []
    for j in range(per):
        copy = pltpu.make_async_copy(part.at[j, base(j, stages)], wg_out.at[j], out_sem.at[1 + j])
        copy.start()
        wg_copies.append(copy)
    for r in range(1, n_t):
        col_copies[r - 1].wait_send()
        for j in range(per):
            gather_copy(r, j).wait_send()
    for j in range(per):
        for b in range(stages):
            reduce_copy(j, b).wait_send()
        wg_copies[j].wait()
    ig_copy.wait()


def finish(n_copies, counts, wg_in, ig_in, wg_out, ig_out, sems):
    per = wg_in.shape[0]
    rows = ig_in.shape[0] // n_copies
    copies = []
    for i in range(n_copies):
        part = pl.ds(i * rows, rows)
        copy = pltpu.make_async_copy(ig_in.at[part], ig_out.at[part], sems.at[i])
        copy.start()
        copies.append(copy)
    first = lax.axis_index("dp") * per
    for j in range(per):
        wg_out[j] = jnp.where(first + j < counts[0], wg_in[j], 0.0)
    for copy in copies:
        copy.wait()


def shards(n_t, n_dp, hidden, out_grad, weights, block_rows, block_cols, counts):
    w = weights[0]
    slots, blk, _ = w.shape
    tokens, width = hidden.shape
    rows = out_grad.shape[0]
    panel = width // blk
    per = slots // n_dp
    stages = n_dp.bit_length() - 1
    anyspace = pl.BlockSpec(memory_space=pl.ANY)
    hbm = pl.BlockSpec(memory_space=pltpu.HBM)
    flops = 4 * slots * tokens * blk * blk
    wg, ig = pl.pallas_call(
        functools.partial(kernel, n_t, n_dp, per, panel),
        out_shape=(
            jax.ShapeDtypeStruct((per, blk, blk), jnp.float32),
            jax.ShapeDtypeStruct((tokens, width), jnp.bfloat16),
        ),
        in_specs=[
            pl.BlockSpec(memory_space=pltpu.SMEM),
            pl.BlockSpec(memory_space=pltpu.SMEM),
            pl.BlockSpec(memory_space=pltpu.VMEM),
            hbm,
            hbm,
            hbm,
        ],
        out_specs=(anyspace, anyspace),
        scratch_shapes=[
            pltpu.VMEM((panel, tokens, blk), jnp.bfloat16),
            pltpu.VMEM((out_grad.shape[1] // blk, rows, blk), jnp.bfloat16),
            pltpu.VMEM(w.shape, jnp.bfloat16),
            pltpu.VMEM((n_t, 1, slots), jnp.int32),
            pltpu.SMEM((n_t, 1, slots), jnp.int32),
            pltpu.SMEM((slots,), jnp.int32),
            pltpu.SMEM((slots,), jnp.int32),
            pltpu.SMEM((panel,), jnp.int32),
            pltpu.VMEM((n_t, slots, rows, blk), jnp.bfloat16),
            pltpu.VMEM((slots, tokens, blk), jnp.bfloat16),
            pltpu.VMEM((per, n_dp, blk, blk), jnp.float32),
            pltpu.VMEM((per, n_dp, blk, blk), jnp.float32),
            pltpu.VMEM((slots + 1, tokens, blk), jnp.float32),
            pltpu.VMEM((tokens, width), jnp.bfloat16),
            pltpu.SemaphoreType.DMA((3,)),
            pltpu.SemaphoreType.DMA((n_t,)),
            pltpu.SemaphoreType.DMA((n_t,)),
            pltpu.SemaphoreType.DMA((n_t,)),
            pltpu.SemaphoreType.DMA((n_t, per)),
            pltpu.SemaphoreType.DMA((n_t, per)),
            pltpu.SemaphoreType.DMA((per, stages)),
            pltpu.SemaphoreType.DMA((per, stages)),
            pltpu.SemaphoreType.DMA((1 + per,)),
        ],
        compiler_params=pltpu.CompilerParams(
            collective_id=0, has_side_effects=True, vmem_limit_bytes=64 * 2**20 - 720 * 2**10
        ),
        cost_estimate=pl.CostEstimate(flops=flops, bytes_accessed=6 * 2**20, transcendentals=0),
    )(counts, block_rows, block_cols, hidden, out_grad, w)
    n_copies = math.gcd(tokens // 16, 12)
    vmem = pl.BlockSpec(memory_space=pltpu.VMEM)
    wg, ig = pl.pallas_call(
        functools.partial(finish, n_copies),
        out_shape=(
            jax.ShapeDtypeStruct((per, blk, blk), jnp.float32),
            jax.ShapeDtypeStruct((tokens, width), jnp.bfloat16),
        ),
        in_specs=[pl.BlockSpec(memory_space=pltpu.SMEM), vmem, hbm],
        out_specs=(vmem, hbm),
        scratch_shapes=[pltpu.SemaphoreType.DMA((n_copies,))],
    )(counts, wg, ig)
    return wg[None], ig


def solution(mesh):
    in_specs = (
        P("dp", "tensor"),
        P(("dp", "tensor"), None),
        P("tensor", None, None, None),
        P("tensor", None),
        P("tensor", None),
        P("tensor"),
    )
    out_specs = (P("tensor", "dp", None, None), P("dp", "tensor"))
    body = functools.partial(shards, mesh.shape["tensor"], mesh.shape["dp"])
    return jax.shard_map(body, mesh=mesh, in_specs=in_specs, out_specs=out_specs, check_vma=False)
```

```python
import functools
import math

import jax
import jax.numpy as jnp
from jax import lax
from jax.experimental import pallas as pl
from jax.experimental.pallas import tpu as pltpu
from jax.sharding import PartitionSpec as P

MESH = pl.DeviceIdType.MESH


def kernel(
    n_t,
    n_dp,
    per,
    panel,
    counts,
    rows_ref,
    cols_ref,
    hid_hbm,
    og_hbm,
    w_hbm,
    wg_out,
    ig_out,
    hid,
    og,
    w,
    allcols,
    cols_sm,
    key,
    before,
    last,
    sbuf,
    gbuf,
    part,
    recv,
    runs,
    ig,
    in_sem,
    sm_sem,
    c_send,
    c_recv,
    g_send,
    g_recv,
    r_send,
    r_recv,
    out_sem,
):
    slots = per * n_dp
    rows = og.shape[1]
    blk = w.shape[1]
    stages = n_dp.bit_length() - 1
    me_t = lax.axis_index("tensor")
    me_d = lax.axis_index("dp")

    w_in = pltpu.make_async_copy(w_hbm, w, in_sem.at[2])

    def load(src, dst, sem):
        def one(c, carry):
            columns = pl.ds(pl.multiple_of(c * blk, blk), blk)
            pltpu.make_async_copy(src.at[:, columns], dst.at[c], sem).start()
            return carry

        lax.fori_loop(0, dst.shape[0], one, 0, unroll=math.gcd(dst.shape[0], 16))

    load(og_hbm, og, in_sem.at[0])

    def peer(r):
        return lax.rem(me_t + r, n_t)

    def source(r):
        return lax.rem(me_t + n_t - r, n_t)

    def bit(b):
        return lax.rem(me_d // (1 << b), 2)

    def bits(j):
        listed = list(range(stages))
        if j % 4 == 1 and stages > 1:
            listed[:2] = [1, 0]
        return listed

    def slot_of(j, q):
        d = 0
        for level, b in enumerate(bits(j)):
            d = d + lax.rem(q // (n_dp >> (level + 1)), 2) * (1 << b)
        return d * per + j

    def partner(b):
        return me_d + (1 << b) * (1 - 2 * bit(b))

    barrier = pltpu.get_barrier_semaphore()
    for r in range(1, n_t):
        pl.semaphore_signal(barrier, inc=1, device_id={"tensor": peer(r)}, device_id_type=MESH)
    for b in range(stages):
        pl.semaphore_signal(barrier, inc=1, device_id={"dp": partner(b)}, device_id_type=MESH)
    pl.semaphore_wait(barrier, n_t - 1 + stages)

    col_copies = []
    for r in range(1, n_t):
        copy = pltpu.make_async_remote_copy(
            src_ref=cols_ref,
            dst_ref=allcols.at[r],
            send_sem=c_send.at[r],
            recv_sem=c_recv.at[r],
            device_id={"tensor": peer(r)},
            device_id_type=MESH,
        )
        copy.start()
        col_copies.append(copy)
    own_cols = pltpu.make_async_copy(cols_ref, cols_sm.at[0], sm_sem.at[0])
    own_cols.start()
    load(hid_hbm, hid, in_sem.at[1])
    w_in.start()
    runs[slots] = jnp.zeros(runs.shape[1:], jnp.float32)
    for r in range(1, n_t):
        col_copies[r - 1].wait_recv()
        pltpu.make_async_copy(allcols.at[r], cols_sm.at[r], sm_sem.at[r]).start()
    for r in range(1, n_t):
        pltpu.make_async_copy(allcols.at[r], cols_sm.at[r], sm_sem.at[r]).wait()
    own_cols.wait()
    pltpu.make_async_copy(og, og, in_sem.at[0]).wait()

    def gather_copy(r, j):
        return pltpu.make_async_remote_copy(
            src_ref=sbuf.at[r, pl.ds(j * n_dp, n_dp)],
            dst_ref=gbuf.at[pl.ds(j * n_dp, n_dp), pl.ds(pl.multiple_of(me_t * rows, 16), rows)],
            send_sem=g_send.at[r, j],
            recv_sem=g_recv.at[r, j],
            device_id={"tensor": peer(r)},
            device_id_type=MESH,
        )

    def block_of(r, j, q):
        return og[cols_sm[r, 0, slot_of(j, q)]]

    order = sorted(range(1, n_t), key=lambda r: -min(r, n_t - r))
    for j in range(per):
        for r in order:

            def pick(q, carry, r=r, j=j):
                sbuf[r, j * n_dp + q] = block_of(n_t - r, j, q)
                return carry

            lax.fori_loop(0, n_dp, pick, 0, unroll=min(n_dp, 8))
            gather_copy(r, j).start()

    for j in range(per):

        def own(q, carry, j=j):
            gbuf[j * n_dp + q, pl.ds(pl.multiple_of(me_t * rows, 16), rows)] = block_of(0, j, q)
            return carry

        lax.fori_loop(0, n_dp, own, 0, unroll=min(n_dp, 8))

    pltpu.make_async_copy(hid, hid, in_sem.at[1]).wait()
    w_in.wait()

    def base(j, level):
        first = 0
        for i, b in enumerate(bits(j)[:level]):
            first = first + bit(b) * (n_dp >> (i + 1))
        return first

    def offset(b):
        return sum(n_dp >> (i + 1) for i in range(b))

    def reduce_copy(j, level):
        half = n_dp >> (level + 1)
        b = bits(j)[level]
        return pltpu.make_async_remote_copy(
            src_ref=part.at[j, pl.ds(base(j, level) + (1 - bit(b)) * half, half)],
            dst_ref=recv.at[j, pl.ds(offset(level), half)],
            send_sem=r_send.at[j, level],
            recv_sem=r_recv.at[j, level],
            device_id={"dp": partner(b)},
            device_id_type=MESH,
        )

    def products(j, first, count):
        def one(i, carry):
            q = first + i
            h = hid[rows_ref[0, slot_of(j, q)]]
            part[j, q] = lax.dot_general(
                h, gbuf[j * n_dp + q], (((0,), (0,)), ((), ())), preferred_element_type=jnp.float32
            )
            return carry

        lax.fori_loop(0, count, one, 0, unroll=min(count, 4))

    def contributions(j):
        def one(q, carry):
            k = j * n_dp + q
            c = lax.dot_general(
                gbuf[k], w[slot_of(j, q)], (((1,), (1,)), ((), ())), preferred_element_type=jnp.float32
            )
            runs[k] = c + runs[before[k]]
            return carry

        lax.fori_loop(0, n_dp, one, 0, unroll=min(n_dp, 4))

    def first_half(j):
        for r in range(1, n_t):
            gather_copy(r, j).wait_recv()
        half = n_dp // 2
        mine = bit(bits(j)[0]) * half
        products(j, half - mine, half)
        reduce_copy(j, 0).start()
        products(j, mine, half)

    def advance(j, level):
        half = n_dp >> (level + 1)
        reduce_copy(j, level).wait_recv()
        mine = base(j, level + 1)

        def add(i, carry):
            part[j, mine + i] = part[j, mine + i] + recv[j, offset(level) + i]
            return carry

        lax.fori_loop(0, half, add, 0, unroll=min(half, 4))
        if level + 1 < stages:
            reduce_copy(j, level + 1).start()

    def search():
        for j in range(per):

            def mark(q, carry, j=j):
                slot = slot_of(j, q)
                key[j * n_dp + q] = jnp.where(slot < counts[0], rows_ref[0, slot], -1)
                return carry

            lax.fori_loop(0, n_dp, mark, 0, unroll=min(n_dp, 8))

        def find_before(k, carry):
            found = slots
            for k2 in range(slots):
                found = jnp.where((key[k2] == key[k]) & (k2 < k), k2, found)
            before[k] = found
            return carry

        lax.fori_loop(0, slots, find_before, 0)

        def find_last(p, carry):
            found = slots
            for k2 in range(slots):
                found = jnp.where(key[k2] == p, k2, found)
            last[p] = found
            return carry

        lax.fori_loop(0, panel, find_last, 0)

    def write_out():
        for p in range(panel):
            ig[:, p * blk : (p + 1) * blk] = runs[last[p]].astype(ig.dtype)

    ig_copy = pltpu.make_async_copy(ig, ig_out, out_sem.at[0])
    for step in range(per + stages):
        if step < per:
            first_half(step)
        if step == 0:
            search()
        if step == per - 1:
            for j in range(per // 2):
                contributions(j)
        for level in reversed(range(stages)):
            j = step - 1 - level
            if 0 <= j < per:
                advance(j, level)
        if step == per - 1:
            for j in range(per // 2, per):
                contributions(j)
            write_out()
            ig_copy.start()
    wg_copies = []
    for j in range(per):
        copy = pltpu.make_async_copy(part.at[j, base(j, stages)], wg_out.at[j], out_sem.at[1 + j])
        copy.start()
        wg_copies.append(copy)
    for r in range(1, n_t):
        col_copies[r - 1].wait_send()
        for j in range(per):
            gather_copy(r, j).wait_send()
    for j in range(per):
        for b in range(stages):
            reduce_copy(j, b).wait_send()
        wg_copies[j].wait()
    ig_copy.wait()


def finish(counts, wg_in, ig_in, wg_out, ig_out):
    per = wg_in.shape[0]
    first = lax.axis_index("dp") * per
    for j in range(per):
        wg_out[j] = jnp.where(first + j < counts[0], wg_in[j], 0.0)
    ig_out[...] = ig_in[...]


def shards(n_t, n_dp, hidden, out_grad, weights, block_rows, block_cols, counts):
    w = weights[0]
    slots, blk, _ = w.shape
    tokens, width = hidden.shape
    rows = out_grad.shape[0]
    panel = width // blk
    per = slots // n_dp
    stages = n_dp.bit_length() - 1
    anyspace = pl.BlockSpec(memory_space=pl.ANY)
    hbm = pl.BlockSpec(memory_space=pltpu.HBM)
    flops = 4 * slots * tokens * blk * blk
    wg, ig = pl.pallas_call(
        functools.partial(kernel, n_t, n_dp, per, panel),
        out_shape=(
            jax.ShapeDtypeStruct((per, blk, blk), jnp.float32),
            jax.ShapeDtypeStruct((tokens, width), jnp.bfloat16),
        ),
        in_specs=[
            pl.BlockSpec(memory_space=pltpu.SMEM),
            pl.BlockSpec(memory_space=pltpu.SMEM),
            pl.BlockSpec(memory_space=pltpu.VMEM),
            hbm,
            hbm,
            hbm,
        ],
        out_specs=(anyspace, anyspace),
        scratch_shapes=[
            pltpu.VMEM((panel, tokens, blk), jnp.bfloat16),
            pltpu.VMEM((out_grad.shape[1] // blk, rows, blk), jnp.bfloat16),
            pltpu.VMEM(w.shape, jnp.bfloat16),
            pltpu.VMEM((n_t, 1, slots), jnp.int32),
            pltpu.SMEM((n_t, 1, slots), jnp.int32),
            pltpu.SMEM((slots,), jnp.int32),
            pltpu.SMEM((slots,), jnp.int32),
            pltpu.SMEM((panel,), jnp.int32),
            pltpu.VMEM((n_t, slots, rows, blk), jnp.bfloat16),
            pltpu.VMEM((slots, tokens, blk), jnp.bfloat16),
            pltpu.VMEM((per, n_dp, blk, blk), jnp.float32),
            pltpu.VMEM((per, n_dp, blk, blk), jnp.float32),
            pltpu.VMEM((slots + 1, tokens, blk), jnp.float32),
            pltpu.VMEM((tokens, width), jnp.bfloat16),
            pltpu.SemaphoreType.DMA((3,)),
            pltpu.SemaphoreType.DMA((n_t,)),
            pltpu.SemaphoreType.DMA((n_t,)),
            pltpu.SemaphoreType.DMA((n_t,)),
            pltpu.SemaphoreType.DMA((n_t, per)),
            pltpu.SemaphoreType.DMA((n_t, per)),
            pltpu.SemaphoreType.DMA((per, stages)),
            pltpu.SemaphoreType.DMA((per, stages)),
            pltpu.SemaphoreType.DMA((1 + per,)),
        ],
        compiler_params=pltpu.CompilerParams(
            collective_id=0, has_side_effects=True, vmem_limit_bytes=64 * 2**20 - 720 * 2**10
        ),
        cost_estimate=pl.CostEstimate(flops=flops, bytes_accessed=6 * 2**20, transcendentals=0),
    )(counts, block_rows, block_cols, hidden, out_grad, w)
    steps = math.gcd(tokens // 16, 4)
    whole = pl.BlockSpec((per, blk, blk), lambda i: (0, 0, 0))
    some = pl.BlockSpec((tokens // steps, width), lambda i: (i, 0))
    wg, ig = pl.pallas_call(
        finish,
        grid=(steps,),
        out_shape=(
            jax.ShapeDtypeStruct((per, blk, blk), jnp.float32),
            jax.ShapeDtypeStruct((tokens, width), jnp.bfloat16),
        ),
        in_specs=[pl.BlockSpec(memory_space=pltpu.SMEM), whole, some],
        out_specs=(whole, some),
    )(counts, wg, ig)
    return wg[None], ig


def solution(mesh):
    in_specs = (
        P("dp", "tensor"),
        P(("dp", "tensor"), None),
        P("tensor", None, None, None),
        P("tensor", None),
        P("tensor", None),
        P("tensor"),
    )
    out_specs = (P("tensor", "dp", None, None), P("dp", "tensor"))
    body = functools.partial(shards, mesh.shape["tensor"], mesh.shape["dp"])
    return jax.shard_map(body, mesh=mesh, in_specs=in_specs, out_specs=out_specs, check_vma=False)
```
